32 devices in a mesh: feat: 8 (over z, x), tgt: 4 (over y, core).
Axes of the slice: x: 2, y: 2, z: 4, core: 2. Of those that a mesh axis runs over, the one named last changes fastest.
Arguments:
- sources: bfloat16 [4, 128, 2304], P('tgt'), may hold values from -6 to 6
- targets: bfloat16 [4, 128, 2304], P('tgt', 'feat'), may hold values from -6 to 6
- enc_weight: bfloat16 [4, 2304, 16384], P('tgt', None, 'feat'), may hold values from -0.125 to 0.125
- enc_bias: float32 [4, 16384], P('tgt', 'feat'), may hold values from -5 to 5
- dec_weight: bfloat16 [4, 4, 16384, 2304], P('tgt', None, 'feat'), may hold values from -0.046875 to 0.046875
- pair_mask: int32 [4, 4], replicated, may hold values from 0 to 1, as said below
Outputs:
- error: bfloat16 [4, 128, 2304], P('tgt', 'feat')
- latent_grad: bfloat16 [4, 128, 16384], P('tgt', None, 'feat')
The draws below stay inside these ranges and needn't reach their ends.
Inputs may be any that keep to these rules, and one draw needn't show every extreme that they name: pair_mask[t, s] is 0 wherever s > t and 1 wherever s == t.
All inputs are finite; a program needn't handle non-finite values.
Results may differ from the reference program's by a relative error of at most 0.0055.
Values may be sent and summed in bfloat16 or wider, within the bound.
A program may use at most 128 MiB of HBM per device.

```python
import jax
import jax.numpy as jnp
from jax import lax

D = 2304
F = 16384
TOK = 128
LAYERS = 4


def draw_pair_mask(key, part):
    picks = jax.random.randint(key, (LAYERS, LAYERS), 0, 4)
    row_ids = lax.broadcasted_iota(jnp.int32, (LAYERS, LAYERS), 0)
    col_ids = lax.broadcasted_iota(jnp.int32, (LAYERS, LAYERS), 1)
    below = jnp.where(picks > 0, 1, 0).astype(jnp.int32)
    return jnp.where(row_ids == col_ids, 1, jnp.where(row_ids > col_ids, below, 0)).astype(jnp.int32)


def block_scale(stream_key, extent, cuts, smallest, top_value):
    factor_of = 1.0
    for dim, parts in cuts:
        draws = jax.random.uniform(jax.random.fold_in(jax.random.fold_in(stream_key, 6), dim), (parts,), jnp.float32, smallest / len(cuts), top_value / len(cuts))
        factor_of = factor_of * jnp.repeat(jnp.exp(draws), extent[dim] // parts).reshape((-1,) + (1,) * (len(extent) - 1 - dim))
    return factor_of


def gaussian(rng, extent, deviation, limit, cuts=(), kind=jnp.bfloat16):
    loudness = block_scale(rng, extent, cuts, -0.22, 0.18) if cuts else 1.0
    result = jax.random.normal(rng, extent, jnp.float32) * deviation * loudness
    return jnp.minimum(jnp.maximum(result, -limit), limit).astype(kind)


def setup_inputs(seed: int = 0) -> dict:
    key_of = jax.random.split(jax.random.key(seed), 7)
    return {
        "sources": gaussian(key_of[0], (LAYERS, TOK, D), 1.0, 6.0, ((0, 4),)),
        "targets": gaussian(key_of[1], (LAYERS, TOK, D), 1.0, 6.0, ((0, 4), (1, 8))),
        "enc_weight": gaussian(key_of[2], (LAYERS, D, F), D ** -0.5, 0.125, ((0, 4), (2, 8))),
        "enc_bias": gaussian(key_of[3], (LAYERS, F), 1.0, 5.0, ((0, 4), (1, 8)), jnp.float32),
        "dec_weight": gaussian(key_of[4], (LAYERS, LAYERS, F, D), F ** -0.5, 0.046875, ((0, 4), (2, 8))),
        "pair_mask": draw_pair_mask(jax.random.fold_in(key_of[6], 71), 0),
    }


def reference(sources, targets, enc_weight, enc_bias, dec_weight, pair_mask):
    latents = []
    for layer in range(LAYERS):
        pre = jnp.dot(sources[layer], enc_weight[layer], preferred_element_type=jnp.float32) + enc_bias[layer]
        latents.append(jnp.maximum(pre, 0.0).astype(jnp.bfloat16))
    errors = []
    for target in range(LAYERS):
        total = jnp.zeros((TOK, D), jnp.float32)
        for source in range(target + 1):
            weight = pair_mask[target, source].astype(jnp.float32)
            total = total + weight * jnp.dot(latents[source], dec_weight[target, source], preferred_element_type=jnp.float32)
        errors.append((total - targets[target].astype(jnp.float32)).astype(jnp.bfloat16))
    grads = []
    for source in range(LAYERS):
        total = jnp.zeros((TOK, F), jnp.float32)
        for target in range(source, LAYERS):
            weight = pair_mask[target, source].astype(jnp.float32)
            term = lax.dot_general(errors[target], dec_weight[target, source], (((1,), (1,)), ((), ())), preferred_element_type=jnp.float32)
            total = total + weight * term
        grads.append(total.astype(jnp.bfloat16))
    return jnp.stack(errors), jnp.stack(grads)
```

```python
import functools
import math

import jax
import jax.numpy as jnp
from jax import lax
from jax.experimental import pallas as pl
from jax.experimental.pallas import tpu as pltpu
from jax.sharding import PartitionSpec as P

MESH = pl.DeviceIdType.MESH
F32 = jnp.float32
BF16 = jnp.bfloat16
PIECES = 4
CHUNKS = 2


def kernel(nf, nt, mask_ref, src_ref, tgt_ref, enc_hbm, bias_ref, dec_hbm, err_ref, grad_ref,
           enc, dec, lat, acc, xsend, xrecv, zsend, zrecv, errbuf, errmat, errkeep,
           ssend, srecv, ysend, yrecv, yown, dsend, drecv, gfin,
           enc_sem, dec_sem, a_recv, a_sib, a_y, a_fwd,
           rx_s, rx_r, rz_s, rz_r, gz_s, gx_s, g_r,
           cs_s, cs_r, cy_s, cy_r, cd_s, cd_r):
    np_, nc, nz = lat.shape[1], xsend.shape[0], nf // 2
    fp = lat.shape[3]
    width = src_ref.shape[2]
    block = tgt_ref.shape[1]
    rows = block // nc
    part = width // nc
    f = lax.axis_index("feat")
    t = lax.axis_index("tgt")
    x, z = lax.rem(f, 2), f // 2
    core, y = lax.rem(t, 2), t // 2
    sib = (f, t + 1 - 2 * core)
    ypeer = (f, lax.rem(t + 2, nt))
    xpeer = (f + 1 - 2 * x, t)

    def zdev(d):
        return lax.rem(z + d, nz)

    def enc_copy(p):
        cols = pl.ds(pl.multiple_of(p * fp, fp), fp)
        return pltpu.make_async_copy(enc_hbm.at[0, :, cols], enc.at[p], enc_sem.at[p])

    def dec_copy(s, p):
        rws = pl.ds(pl.multiple_of(p * fp, fp), fp)
        return pltpu.make_async_copy(dec_hbm.at[0, s, rws, :], dec.at[s, p], dec_sem.at[s, p])

    def remote(src, dst, ss, rs, dev):
        return pltpu.make_async_remote_copy(
            src_ref=src, dst_ref=dst, send_sem=ss, recv_sem=rs, device_id=dev, device_id_type=MESH)

    def each(body, n=np_):
        def step(i, carry):
            body(i)
            return carry
        lax.fori_loop(0, n, step, 0)

    each(lambda p: enc_copy(p).start())
    each(lambda p: dec_copy(t, p).start())

    @pl.when(core == 1)
    def _():
        each(lambda p: dec_copy(t - 1, p).start())

    @pl.when(y == 1)
    def _():
        def go(p):
            dec_copy(core, p).start()
            dec_copy(1 - core, p).start()
        each(go)

    barrier = pltpu.get_barrier_semaphore()
    peers = [sib, ypeer, xpeer] + [(zdev(d) * 2 + x, t) for d in range(1, nz)]
    for dev in peers:
        pl.semaphore_signal(barrier, inc=1, device_id=dev, device_id_type=MESH)
    pl.semaphore_wait(barrier, len(peers))

    def lat_to_sib(p):
        return remote(lat.at[t, p], lat.at[t, p], a_sib.at[p], a_recv.at[t, p], sib)

    def lat_to_y(p):
        return remote(lat.at[t, p], lat.at[t, p], a_y.at[p], a_recv.at[t, p], ypeer)

    def lat_forward(p):
        return remote(lat.at[core, p], lat.at[core, p], a_fwd.at[p], a_recv.at[core, p], sib)

    def lat_wait(s, p):
        remote(lat.at[s, p], lat.at[s, p], a_fwd.at[p], a_recv.at[s, p], sib).wait_recv()

    def encode(p):
        enc_copy(p).wait()
        pre = jnp.dot(src_ref[0], enc[p], preferred_element_type=F32)
        cols = pl.ds(pl.multiple_of(p * fp, fp), fp)
        lat[t, p] = jnp.maximum(pre + bias_ref[:, cols], 0.0).astype(BF16)

        @pl.when(y == 0)
        def _():
            lat_to_y(p).start()

        @pl.when(core == 0)
        def _():
            lat_to_sib(p).start()
    each(encode)

    def decode(s, p, first=False):
        dec_copy(s, p).wait()
        scale = mask_ref[t, s].astype(F32).astype(BF16)
        left = lat[s, p] * scale
        step = 256 if width % 256 == 0 else 128
        for n in range(0, width, step):
            got = jnp.dot(left, dec[s, p, :, n:n + step], preferred_element_type=F32)
            if first:
                acc[:, n:n + step] = got
            else:
                acc[:, n:n + step] += got

    decode(t, 0, True)
    each(lambda i: decode(t, i + 1), np_ - 1)

    @pl.when(core == 1)
    def _():
        def go(p):
            lat_wait(t - 1, p)
            decode(t - 1, p)
        each(go)

    @pl.when(y == 1)
    def _():
        lat_wait(core, 0)
        lat_forward(0).start()
        decode(core, 0)

        def go(i):
            lat_wait(core, i + 1)
            lat_forward(i + 1).start()
            decode(core, i + 1)
            lat_wait(1 - core, i)
            decode(1 - core, i)
        each(go, np_ - 1)
        lat_wait(1 - core, np_ - 1)
        decode(1 - core, np_ - 1)

    def pack(v):
        if nc == 1:
            return v.astype(BF16)
        return jnp.concatenate([v[:, j * part:(j + 1) * part] for j in range(nc)], axis=0).astype(BF16)

    def unpack(v):
        v = v.astype(F32)
        if nc == 1:
            return v
        return jnp.concatenate([v[j * rows:(j + 1) * rows] for j in range(nc)], axis=1)

    def mine(c, g):
        return acc[pl.ds(pl.multiple_of(g * block + c * rows, rows), rows), :]

    def rx(c, k):
        return remote(xsend.at[c, k], xrecv.at[c, k], rx_s.at[c, k], rx_r.at[c, k], xpeer)

    def rz(c, d):
        to = zdev(d)
        return remote(zsend.at[c, to], zrecv.at[c, z], rz_s.at[c, to], rz_r.at[c, z], (to * 2 + x, t))

    def rz_wait(c, d):
        fr = zdev(d)
        remote(zsend.at[c, fr], zrecv.at[c, fr], rz_s.at[c, fr], rz_r.at[c, fr], xpeer).wait_recv()

    def sum_x(c):
        for d in list(range(1, nz)) + [0]:
            k = zdev(d)
            xsend[c, k] = pack(mine(c, k * 2 + 1 - x))
            rx(c, k).start()

    def sum_z(c):
        for d in range(1, nz):
            k = zdev(d)
            rx(c, k).wait_recv()
            zsend[c, k] = pack(mine(c, k * 2 + x) + unpack(xrecv[c, k]))
            rz(c, d).start()

    def gather_z(c, d):
        return remote(errbuf.at[c, f], errbuf.at[c, f], gz_s.at[c, d - 1], g_r.at[c, f], (zdev(d) * 2 + x, t))

    def gather_x(c, k):
        g = k * 2 + x
        return remote(errbuf.at[c, g], errbuf.at[c, g], gx_s.at[c, k], g_r.at[c, g], xpeer)

    def gather_wait(c, g):
        remote(errbuf.at[c, g], errbuf.at[c, g], gx_s.at[c, 0], g_r.at[c, g], xpeer).wait_recv()

    def finish(c):
        rx(c, z).wait_recv()
        total = mine(c, z * 2 + x) + unpack(xrecv[c, z])
        for d in range(1, nz):
            rz_wait(c, d)
            total = total + unpack(zrecv[c, zdev(d)])
        err = total - tgt_ref[0].astype(F32)[c * rows:(c + 1) * rows]
        errkeep[pl.ds(c * rows, rows), :] = err
        errbuf[c, f] = pack(err)
        for d in range(1, nz):
            gather_z(c, d).start()
        gather_x(c, z).start()

    def forward(c):
        for d in range(1, nz):
            k = zdev(d)
            gather_wait(c, k * 2 + x)
            gather_x(c, k).start()

    def collect(c):
        for d in range(nz):
            gather_wait(c, zdev(d) * 2 + 1 - x)
        group = math.lcm(rows, 16) // rows
        for g in range(0, nf, group):
            value = jnp.concatenate([unpack(errbuf[c, g + j]) for j in range(group)], axis=0)
            errmat[c, g * rows:(g + group) * rows, :] = value.astype(BF16)

    def term(c, s, p):
        scale = mask_ref[t, s].astype(F32)
        return scale * lax.dot_general(
            errmat[c], dec[s, p], (((1,), (1,)), ((), ())), preferred_element_type=F32)

    def to_sib(c, p):
        return remote(ssend.at[c, p], srecv.at[c, p], cs_s.at[c, p], cs_r.at[c, p], sib)

    def to_y(c, p):
        return remote(ysend.at[c, p], yrecv.at[c, p], cy_s.at[c, p], cy_r.at[c, p], ypeer)

    def down(c, p):
        return remote(dsend.at[c, p], drecv.at[c, p], cd_s.at[c, p], cd_r.at[c, p], sib)

    def grads_y(c):
        @pl.when(y == 1)
        def _():
            def give(p):
                ssend[c, p] = term(c, 1 - core, p).astype(BF16)
                to_sib(c, p).start()
                yown[p] = term(c, core, p)

            def pass_on(p):
                to_sib(c, p).wait_recv()
                ysend[c, p] = (yown[p] + srecv[c, p].astype(F32)).astype(BF16)
                to_y(c, p).start()

            give(0)

            def go(i):
                give(i + 1)
                pass_on(i)
            each(go, np_ - 1)
            pass_on(np_ - 1)

    def grads_pair(c):
        @pl.when(core == 1)
        def _():
            def go(p):
                dsend[c, p] = term(c, t - 1, p).astype(BF16)
                down(c, p).start()
            each(go)

        def own(p):
            gfin[c, p] = term(c, t, p)
        each(own)

    def land(p):
        @pl.when(core == 0)
        def _():
            for c in range(nc):
                down(c, p).wait_recv()
                gfin[c, p] += drecv[c, p].astype(F32)

        @pl.when(y == 0)
        def _():
            for c in range(nc):
                to_y(c, p).wait_recv()
                gfin[c, p] += yrecv[c, p].astype(F32)
        cols = pl.ds(pl.multiple_of(p * fp, fp), fp)
        for g in range(nf):
            value = jnp.concatenate([gfin[c, p, g * rows:(g + 1) * rows, :] for c in range(nc)], axis=0)
            grad_ref[0, g * block:(g + 1) * block, cols] = value.astype(BF16)

    sum_x(0)
    sum_z(0)
    for c in range(1, nc):
        sum_x(c)
    for c in range(nc):
        finish(c)
        if c + 1 < nc:
            sum_z(c + 1)
        if c == 0:
            forward(0)
    collect(0)
    grads_y(0)
    for c in range(1, nc):
        forward(c)
        collect(c)
        grads_y(c)
    for c in range(nc):
        grads_pair(c)
    err_ref[0] = errkeep[...].astype(BF16)
    each(land)

    def drain(p):
        @pl.when(y == 0)
        def _():
            lat_to_y(p).wait_send()

        @pl.when(core == 0)
        def _():
            lat_to_sib(p).wait_send()

        @pl.when(y == 1)
        def _():
            lat_forward(p).wait_send()
            for c in range(nc):
                to_sib(c, p).wait_send()
                to_y(c, p).wait_send()

        @pl.when(core == 1)
        def _():
            for c in range(nc):
                down(c, p).wait_send()
    each(drain)
    for c in range(nc):
        for d in range(nz):
            rx(c, zdev(d)).wait_send()
            gather_x(c, zdev(d)).wait_send()
            if d:
                rz(c, d).wait_send()
                gather_z(c, d).wait_send()


def fused(nf, nt, sources, targets, enc_weight, enc_bias, dec_weight, pair_mask):
    tok, width = sources.shape[1:]
    local = enc_weight.shape[2]
    layers = dec_weight.shape[1]
    block = targets.shape[1]
    np_, nc, nz = PIECES, CHUNKS, nf // 2
    fp = local // np_
    half = tok // nc
    part = width // nc
    vm = pltpu.VMEM
    dma = pltpu.SemaphoreType.DMA
    anywhere = pl.BlockSpec(memory_space=pl.ANY)
    inside = pl.BlockSpec(memory_space=pltpu.VMEM)
    piece = (nc, np_, half, fp)
    return pl.pallas_call(
        functools.partial(kernel, nf, nt),
        out_shape=(
            jax.ShapeDtypeStruct(targets.shape, BF16),
            jax.ShapeDtypeStruct((1, tok, local), BF16),
        ),
        in_specs=[pl.BlockSpec(memory_space=pltpu.SMEM), inside, inside, anywhere, inside, anywhere],
        out_specs=(inside, inside),
        scratch_shapes=[
            vm((np_, width, fp), BF16),
            vm((layers, np_, fp, width), BF16),
            vm((layers, np_, tok, fp), BF16),
            vm((tok, width), F32),
            vm((nc, nz, block, part), BF16),
            vm((nc, nz, block, part), BF16),
            vm((nc, nz, block, part), BF16),
            vm((nc, nz, block, part), BF16),
            vm((nc, nf, block, part), BF16),
            vm((nc, half, width), BF16),
            vm((block, width), F32),
            vm(piece, BF16), vm(piece, BF16), vm(piece, BF16), vm(piece, BF16),
            vm((np_, half, fp), F32),
            vm(piece, BF16), vm(piece, BF16),
            vm(piece, F32),
            dma((np_,)), dma((layers, np_)), dma((layers, np_)), dma((np_,)), dma((np_,)), dma((np_,)),
            dma((nc, nz)), dma((nc, nz)), dma((nc, nz)), dma((nc, nz)),
            dma((nc, nz)), dma((nc, nz)), dma((nc, nf)),
            dma((nc, np_)), dma((nc, np_)), dma((nc, np_)), dma((nc, np_)), dma((nc, np_)), dma((nc, np_)),
        ],
        compiler_params=pltpu.CompilerParams(
            collective_id=0, has_side_effects=True, vmem_limit_bytes=63 * 1024 * 1024),
        cost_estimate=pl.CostEstimate(
            flops=2 * tok * width * local * (1 + 2 * layers),
            bytes_accessed=2 * width * local * (1 + layers), transcendentals=0),
    )(pair_mask, sources, targets, enc_weight, enc_bias, dec_weight)


def fits(nf, nt, tok, width, local, layers):
    block = tok // nf
    return (
        nt == 4 and layers == 4 and nf % 2 == 0 and tok % nf == 0 and block % 16 == 0
        and local % (PIECES * 128) == 0 and width % (CHUNKS * 128) == 0
        and 2 * width * local * (1 + layers) + 14 * tok * local * 2 <= 56 * 1024 * 1024
    )


def per_device(sources, targets, enc_weight, enc_bias, dec_weight, pair_mask):
    layer_count = dec_weight.shape[1]
    tok_total = sources.shape[1]
    width = sources.shape[2]
    rows_local = targets.shape[1]
    pre = jnp.dot(sources[0], enc_weight[0], preferred_element_type=jnp.float32) + enc_bias[0]
    latent = jnp.maximum(pre, 0.0).astype(jnp.bfloat16)
    latent_all = lax.all_gather(latent[None], "tgt", axis=0, tiled=True)
    owner = lax.axis_index("tgt")
    mask_row = lax.dynamic_index_in_dim(pair_mask, owner, 0, keepdims=False)
    total = jnp.zeros((tok_total, width), jnp.float32)
    for recon_source in range(layer_count):
        rows = latent_all[recon_source]
        recon_weight = mask_row[recon_source].astype(jnp.float32)
        total = total + recon_weight * jnp.dot(
            rows, dec_weight[0, recon_source], preferred_element_type=jnp.float32
        )
    whole = lax.psum(total, "feat")
    target_full = lax.all_gather(targets[0], "feat", axis=0, tiled=True)
    err_full = (whole - target_full.astype(jnp.float32)).astype(jnp.bfloat16)
    err_local = lax.dynamic_slice_in_dim(
        err_full, lax.axis_index("feat") * rows_local, rows_local, 0
    )
    terms = []
    for source in range(layer_count):
        weight = mask_row[source].astype(jnp.float32)
        term = weight * lax.dot_general(
            err_full,
            dec_weight[0, source],
            (((1,), (1,)), ((), ())),
            preferred_element_type=jnp.float32,
        )
        terms.append(term)
    stacked = jnp.stack(terms)
    grads = lax.psum_scatter(stacked, "tgt", scatter_dimension=0, tiled=True)
    return (err_local[None], grads.astype(jnp.bfloat16))


def solution(mesh):
    in_specs = (
        P("tgt", None, None),
        P("tgt", "feat", None),
        P("tgt", None, "feat"),
        P("tgt", "feat"),
        P("tgt", None, "feat", None),
        P(),
    )
    out_specs = (P("tgt", "feat", None), P("tgt", None, "feat"))
    nf, nt = mesh.shape["feat"], mesh.shape["tgt"]

    def local(sources, targets, enc_weight, enc_bias, dec_weight, pair_mask):
        tok, width = sources.shape[1:]
        args = (sources, targets, enc_weight, enc_bias, dec_weight, pair_mask)
        if fits(nf, nt, tok, width, enc_weight.shape[2], dec_weight.shape[1]):
            return fused(nf, nt, *args)
        return per_device(*args)

    return jax.shard_map(
        local, mesh=mesh, in_specs=in_specs, out_specs=out_specs, check_vma=False
    )
```

```python
import functools
import math

import jax
import jax.numpy as jnp
from jax import lax
from jax.experimental import pallas as pl
from jax.experimental.pallas import tpu as pltpu
from jax.sharding import PartitionSpec as P

MESH = pl.DeviceIdType.MESH
F32 = jnp.float32
BF16 = jnp.bfloat16
PIECES = 4
CHUNKS = 2
WINDOW = 4
SWAP = False


def kernel(nf, nt, mask_ref, src_ref, tgt_ref, enc_hbm, bias_ref, dec_hbm, err_ref, grad_ref,
           enc, dec, lat, acc, xsend, xrecv, zsend, zrecv, errbuf, errmat,
           ssend, srecv, ysend, yrecv, yown, dsend, drecv, gfin,
           enc_sem, dec_sem, a_recv, a_sib, a_y, a_fwd,
           rx_s, rx_r, rz_s, rz_r, gz_s, gx_s, g_r,
           cs_s, cs_r, cy_s, cy_r, cd_s, cd_r):
    np_, nc, nz = lat.shape[1], xsend.shape[0], nf // 2
    fp = lat.shape[3]
    width = src_ref.shape[2]
    block = tgt_ref.shape[1]
    part = width // nc
    f = lax.axis_index("feat")
    t = lax.axis_index("tgt")
    x, z = lax.rem(f, 2), f // 2
    core, y = lax.rem(t, 2), t // 2
    sib = (f, t + 1 - 2 * core)
    ypeer = (f, lax.rem(t + 2, nt))
    xpeer = (f + 1 - 2 * x, t)

    def zdev(d):
        return lax.rem(z + d, nz)

    def enc_copy(p):
        cols = pl.ds(pl.multiple_of(p * fp, fp), fp)
        return pltpu.make_async_copy(enc_hbm.at[0, :, cols], enc.at[p], enc_sem.at[p])

    def dec_copy(s, p):
        rws = pl.ds(pl.multiple_of(p * fp, fp), fp)
        return pltpu.make_async_copy(dec_hbm.at[0, s, rws, :], dec.at[s, p], dec_sem.at[s, p])

    def remote(src, dst, ss, rs, dev):
        return pltpu.make_async_remote_copy(
            src_ref=src, dst_ref=dst, send_sem=ss, recv_sem=rs, device_id=dev, device_id_type=MESH)

    def each(body, n=np_):
        def step(i, carry):
            body(i)
            return carry
        lax.fori_loop(0, n, step, 0)

    each(lambda p: enc_copy(p).start())
    each(lambda p: dec_copy(t, p).start())

    @pl.when(core == 1)
    def _():
        each(lambda p: dec_copy(t - 1, p).start())

    @pl.when(y == 1)
    def _():
        def go(p):
            dec_copy(core, p).start()
            dec_copy(1 - core, p).start()
        each(go)

    barrier = pltpu.get_barrier_semaphore()
    peers = [sib, ypeer, xpeer] + [(zdev(d) * 2 + x, t) for d in range(1, nz)]
    for dev in peers:
        pl.semaphore_signal(barrier, inc=1, device_id=dev, device_id_type=MESH)
    pl.semaphore_wait(barrier, len(peers))

    def lat_to_sib(p):
        return remote(lat.at[t, p], lat.at[t, p], a_sib.at[p], a_recv.at[t, p], sib)

    def lat_to_y(p):
        return remote(lat.at[t, p], lat.at[t, p], a_y.at[p], a_recv.at[t, p], ypeer)

    def lat_forward(p):
        return remote(lat.at[core, p], lat.at[core, p], a_fwd.at[p], a_recv.at[core, p], sib)

    def lat_wait(s, p):
        remote(lat.at[s, p], lat.at[s, p], a_fwd.at[p], a_recv.at[s, p], sib).wait_recv()

    def encode(p):
        enc_copy(p).wait()
        pre = jnp.dot(src_ref[0], enc[p], preferred_element_type=F32)
        cols = pl.ds(pl.multiple_of(p * fp, fp), fp)
        lat[t, p] = jnp.maximum(pre + bias_ref[:, cols], 0.0).astype(BF16)

        @pl.when(y == 0)
        def _():
            lat_to_y(p).start()

        @pl.when(core == 0)
        def _():
            lat_to_sib(p).start()
    each(encode)

    def decode(s, p, first=False):
        dec_copy(s, p).wait()
        scale = mask_ref[t, s].astype(F32).astype(BF16)
        left = lat[s, p] * scale
        step = 256 if width % 256 == 0 else 128
        for n in range(0, width, step):
            got = jnp.dot(left, dec[s, p, :, n:n + step], preferred_element_type=F32)
            if first:
                acc[:, n:n + step] = got
            else:
                acc[:, n:n + step] += got

    decode(t, 0, True)
    each(lambda i: decode(t, i + 1), np_ - 1)

    @pl.when(core == 1)
    def _():
        def go(p):
            lat_wait(t - 1, p)
            decode(t - 1, p)
        each(go)

    @pl.when(y == 1)
    def _():
        lat_wait(core, 0)
        lat_forward(0).start()
        decode(core, 0)

        def go(i):
            lat_wait(core, i + 1)
            lat_forward(i + 1).start()
            decode(core, i + 1)
            lat_wait(1 - core, i)
            decode(1 - core, i)
        each(go, np_ - 1)
        lat_wait(1 - core, np_ - 1)
        decode(1 - core, np_ - 1)

    def mine(c, g):
        return acc[pl.ds(pl.multiple_of(g * block, block), block), c * part:(c + 1) * part]

    def rx(c, k):
        return remote(xsend.at[c, k], xrecv.at[c, k], rx_s.at[c, k], rx_r.at[c, k], xpeer)

    def rz(c, d):
        to = zdev(d)
        return remote(zsend.at[c, to], zrecv.at[c, z], rz_s.at[c, to], rz_r.at[c, z], (to * 2 + x, t))

    def rz_wait(c, d):
        fr = zdev(d)
        remote(zsend.at[c, fr], zrecv.at[c, fr], rz_s.at[c, fr], rz_r.at[c, fr], xpeer).wait_recv()

    def sum_feat():
        order = [(c, d) for c in range(nc) for d in list(range(1, nz)) + [0]]

        def take(i):
            c, d = order[i]
            k = zdev(d)
            rx(c, k).wait_recv()
            if d:
                zsend[c, k] = (mine(c, k * 2 + x) + xrecv[c, k].astype(F32)).astype(BF16)
                rz(c, d).start()

        for i, (c, d) in enumerate(order):
            k = zdev(d)
            xsend[c, k] = mine(c, k * 2 + 1 - x).astype(BF16)
            if i >= WINDOW:
                rx(order[i - WINDOW][0], zdev(order[i - WINDOW][1])).wait_send()
            rx(c, k).start()
            if i >= WINDOW - 1:
                take(i - WINDOW + 1)
        for i in range(len(order) - WINDOW + 1, len(order)):
            take(i)
        for c, d in order[-WINDOW:]:
            rx(c, zdev(d)).wait_send()

    def gather_z(c, d):
        return remote(errbuf.at[c, f], errbuf.at[c, f], gz_s.at[c, d - 1], g_r.at[c, f], (zdev(d) * 2 + x, t))

    def gather_x(c, k):
        g = k * 2 + x
        return remote(errbuf.at[c, g], errbuf.at[c, g], gx_s.at[c, k], g_r.at[c, g], xpeer)

    def gather_wait(c, g):
        remote(errbuf.at[c, g], errbuf.at[c, g], gx_s.at[c, 0], g_r.at[c, g], xpeer).wait_recv()

    near = sorted(range(1, nz), key=lambda d: min(d, nz - d))

    def finish(c):
        total = mine(c, z * 2 + x) + xrecv[c, z].astype(F32)
        for d in range(1, nz):
            rz_wait(c, d)
            total = total + zrecv[c, zdev(d)].astype(F32)
        cols = slice(c * part, (c + 1) * part)
        err = (total - tgt_ref[0, :, cols].astype(F32)).astype(BF16)
        err_ref[0, :, cols] = err
        errbuf[c, f] = err
        gather_x(c, z).start()
        for i, d in enumerate(near):
            gather_z(c, d).start()

    def forward(c):
        for d in near:
            k = zdev(d)
            gather_wait(c, k * 2 + x)
            gather_x(c, k).start()

    def collect(c):
        for d in range(nz):
            gather_wait(c, zdev(d) * 2 + 1 - x)
        cols = slice(c * part, (c + 1) * part)
        if SWAP:
            value = jnp.concatenate([errbuf[c, g] for g in range(nf)], axis=0)
            errmat[cols, :] = value.astype(F32).T.astype(BF16)
        else:
            for g in range(nf):
                errmat[g * block:(g + 1) * block, cols] = errbuf[c, g]

    def term(s, p):
        scale = mask_ref[t, s].astype(F32)
        if SWAP:
            return scale * jnp.dot(dec[s, p], errmat[...], preferred_element_type=F32)
        return scale * lax.dot_general(
            errmat[...], dec[s, p], (((1,), (1,)), ((), ())), preferred_element_type=F32)

    def to_sib(p):
        return remote(ssend.at[p], srecv.at[p], cs_s.at[p], cs_r.at[p], sib)

    def to_y(p):
        return remote(ysend.at[p], yrecv.at[p], cy_s.at[p], cy_r.at[p], ypeer)

    def down(p):
        return remote(dsend.at[p], drecv.at[p], cd_s.at[p], cd_r.at[p], sib)

    def grads_y():
        @pl.when(y == 1)
        def _():
            def give(p):
                ssend[p] = term(1 - core, p).astype(BF16)
                to_sib(p).start()
                yown[p] = term(core, p)

            def pass_on(p):
                to_sib(p).wait_recv()
                ysend[p] = (yown[p] + srecv[p].astype(F32)).astype(BF16)
                to_y(p).start()

            give(0)

            def go(i):
                give(i + 1)
                pass_on(i)
            each(go, np_ - 1)
            pass_on(np_ - 1)

    def grads_pair():
        @pl.when(core == 1)
        def _():
            def go(p):
                dsend[p] = term(t - 1, p).astype(BF16)
                down(p).start()
            each(go)

        def own(p):
            gfin[p] = term(t, p)
        each(own)

    def land(p):
        @pl.when(core == 0)
        def _():
            down(p).wait_recv()
            gfin[p] += drecv[p].astype(F32)

        @pl.when(y == 0)
        def _():
            to_y(p).wait_recv()
            gfin[p] += yrecv[p].astype(F32)
        cols = pl.ds(pl.multiple_of(p * fp, fp), fp)
        value = gfin[p].T if SWAP else gfin[p]
        grad_ref[0, :, cols] = value.astype(BF16)

    sum_feat()
    for c in range(nc):
        finish(c)
    for c in range(nc):
        forward(c)
    for c in range(nc):
        collect(c)
    grads_y()
    grads_pair()
    each(land)

    def drain(p):
        @pl.when(y == 0)
        def _():
            lat_to_y(p).wait_send()

        @pl.when(core == 0)
        def _():
            lat_to_sib(p).wait_send()

        @pl.when(y == 1)
        def _():
            lat_forward(p).wait_send()
            to_sib(p).wait_send()
            to_y(p).wait_send()

        @pl.when(core == 1)
        def _():
            down(p).wait_send()
    each(drain)
    for c in range(nc):
        for d in range(nz):
            gather_x(c, zdev(d)).wait_send()
            if d:
                rz(c, d).wait_send()
        for d in near:
            gather_z(c, d).wait_send()


def fused(nf, nt, sources, targets, enc_weight, enc_bias, dec_weight, pair_mask):
    tok, width = sources.shape[1:]
    local = enc_weight.shape[2]
    layers = dec_weight.shape[1]
    block = targets.shape[1]
    np_, nc, nz = PIECES, CHUNKS, nf // 2
    fp = local // np_
    part = width // nc
    vm = pltpu.VMEM
    dma = pltpu.SemaphoreType.DMA
    anywhere = pl.BlockSpec(memory_space=pl.ANY)
    inside = pl.BlockSpec(memory_space=pltpu.VMEM)
    piece = (np_, fp, tok) if SWAP else (np_, tok, fp)
    return pl.pallas_call(
        functools.partial(kernel, nf, nt),
        out_shape=(
            jax.ShapeDtypeStruct(targets.shape, BF16),
            jax.ShapeDtypeStruct((1, tok, local), BF16),
        ),
        in_specs=[pl.BlockSpec(memory_space=pltpu.SMEM), inside, inside, anywhere, inside, anywhere],
        out_specs=(inside, inside),
        scratch_shapes=[
            vm((np_, width, fp), BF16),
            vm((layers, np_, fp, width), BF16),
            vm((layers, np_, tok, fp), BF16),
            vm((tok, width), F32),
            vm((nc, nz, block, part), BF16),
            vm((nc, nz, block, part), BF16),
            vm((nc, nz, block, part), BF16),
            vm((nc, nz, block, part), BF16),
            vm((nc, nf, block, part), BF16),
            vm((width, tok) if SWAP else (tok, width), BF16),
            vm(piece, BF16), vm(piece, BF16), vm(piece, BF16), vm(piece, BF16),
            vm(piece, F32),
            vm(piece, BF16), vm(piece, BF16),
            vm(piece, F32),
            dma((np_,)), dma((layers, np_)), dma((layers, np_)), dma((np_,)), dma((np_,)), dma((np_,)),
            dma((nc, nz)), dma((nc, nz)), dma((nc, nz)), dma((nc, nz)),
            dma((nc, nz)), dma((nc, nz)), dma((nc, nf)),
            dma((np_,)), dma((np_,)), dma((np_,)), dma((np_,)), dma((np_,)), dma((np_,)),
        ],
        compiler_params=pltpu.CompilerParams(
            collective_id=0, has_side_effects=True, vmem_limit_bytes=63 * 1024 * 1024),
        cost_estimate=pl.CostEstimate(
            flops=2 * tok * width * local * (1 + 2 * layers),
            bytes_accessed=2 * width * local * (1 + layers), transcendentals=0),
    )(pair_mask, sources, targets, enc_weight, enc_bias, dec_weight)


def fits(nf, nt, tok, width, local, layers):
    block = tok // nf
    return (
        nt == 4 and layers == 4 and nf % 2 == 0 and tok % nf == 0 and block % 16 == 0
        and local % (PIECES * 128) == 0 and width % (CHUNKS * 128) == 0
        and 2 * width * local * (1 + layers) + 14 * tok * local * 2 <= 56 * 1024 * 1024
    )


def per_device(sources, targets, enc_weight, enc_bias, dec_weight, pair_mask):
    layer_count = dec_weight.shape[1]
    tok_total = sources.shape[1]
    width = sources.shape[2]
    rows_local = targets.shape[1]
    pre = jnp.dot(sources[0], enc_weight[0], preferred_element_type=jnp.float32) + enc_bias[0]
    latent = jnp.maximum(pre, 0.0).astype(jnp.bfloat16)
    latent_all = lax.all_gather(latent[None], "tgt", axis=0, tiled=True)
    owner = lax.axis_index("tgt")
    mask_row = lax.dynamic_index_in_dim(pair_mask, owner, 0, keepdims=False)
    total = jnp.zeros((tok_total, width), jnp.float32)
    for recon_source in range(layer_count):
        rows = latent_all[recon_source]
        recon_weight = mask_row[recon_source].astype(jnp.float32)
        total = total + recon_weight * jnp.dot(
            rows, dec_weight[0, recon_source], preferred_element_type=jnp.float32
        )
    whole = lax.psum(total, "feat")
    target_full = lax.all_gather(targets[0], "feat", axis=0, tiled=True)
    err_full = (whole - target_full.astype(jnp.float32)).astype(jnp.bfloat16)
    err_local = lax.dynamic_slice_in_dim(
        err_full, lax.axis_index("feat") * rows_local, rows_local, 0
    )
    terms = []
    for source in range(layer_count):
        weight = mask_row[source].astype(jnp.float32)
        term = weight * lax.dot_general(
            err_full,
            dec_weight[0, source],
            (((1,), (1,)), ((), ())),
            preferred_element_type=jnp.float32,
        )
        terms.append(term)
    stacked = jnp.stack(terms)
    grads = lax.psum_scatter(stacked, "tgt", scatter_dimension=0, tiled=True)
    return (err_local[None], grads.astype(jnp.bfloat16))


def solution(mesh):
    in_specs = (
        P("tgt", None, None),
        P("tgt", "feat", None),
        P("tgt", None, "feat"),
        P("tgt", "feat"),
        P("tgt", None, "feat", None),
        P(),
    )
    out_specs = (P("tgt", "feat", None), P("tgt", None, "feat"))
    nf, nt = mesh.shape["feat"], mesh.shape["tgt"]

    def local(sources, targets, enc_weight, enc_bias, dec_weight, pair_mask):
        tok, width = sources.shape[1:]
        args = (sources, targets, enc_weight, enc_bias, dec_weight, pair_mask)
        if fits(nf, nt, tok, width, enc_weight.shape[2], dec_weight.shape[1]):
            return fused(nf, nt, *args)
        return per_device(*args)

    return jax.shard_map(
        local, mesh=mesh, in_specs=in_specs, out_specs=out_specs, check_vma=False
    )
```
